128 devices in a mesh: doc: 8 (over y, x_hi), cent: 16 (over z, x_lo, core).
Axes of the slice: x: 4 (x_hi: 2, x_lo: 2; x = x_hi * 2 + x_lo), y: 4, z: 4, core: 2. Of those that a mesh axis runs over, the one named last changes fastest.
Arguments:
- embeddings: float32 [65536, 1024], P(('doc', 'cent'))
- centroids: float32 [16384, 1024], P('cent')
- cluster: int32 [65536], P(('doc', 'cent')), may hold values from 0 to 16383, as said below
- slot: int32 [65536], P(('doc', 'cent')), may hold values from 0 to 7, as said below
Outputs:
- soft_cost: float32 [65536], P(('doc', 'cent'))
- dup_sim: float32 [65536], P(('doc', 'cent'))
The draws below stay inside these ranges and needn't reach their ends.
Inputs may be any that keep to these rules, and one draw needn't show every extreme that they name: Owner device of row r is cluster[r] // 128; some owner device receives rows from every device. `slot`: slots of the rows of one device that have the same owner device are distinct; in every draw some owner device takes 8 rows from every device.
All inputs are finite; a program needn't handle non-finite values.
Results may differ from the reference program's by a relative error of at most 0.0003.
Values may be sent and summed in bfloat16 or wider, within the bound.
No kernel may reach another device: no remote copies, remote signals or barrier semaphores. Data moves between devices by JAX's collectives and lax.ppermute only.
A program may use at most 192 MiB of HBM per device.

```python
import jax
import jax.numpy as jnp
from jax import lax

D = 1024
ROW_DEV = 512
K = 16384
ROWS = 65536
CL_DEV = 128
CAP = 8
N_DOC = 8
N_CENT = 16


def centroid_table(key):
    base = jax.random.fold_in(key, 1)
    table = jax.random.normal(base, (K, D), jnp.float32)
    return table


def draw_centroids(key, part):
    return centroid_table(key)


def draw_embeddings(key, part):
    noise = jax.random.normal(jax.random.fold_in(key, 2), (ROWS, D), jnp.float32)
    scale = jnp.exp(jax.random.uniform(jax.random.fold_in(key, 3), (ROWS, 1), jnp.float32, 0.0, jnp.log(16.0)))
    return (noise * scale).astype(jnp.float32)


def route_table(key):
    devices = ROWS // ROW_DEV
    slots = 2 * ROW_DEV
    level = jax.random.randint(jax.random.fold_in(key, 20), (devices,), 0, 4)
    hottest = jax.random.randint(jax.random.fold_in(key, 21), (), 0, devices)
    index = jnp.arange(slots, dtype=jnp.int32)
    owner_of = index // CAP
    noise = jax.random.randint(jax.random.fold_in(key, 22), (devices, slots), 0, 1024)
    score = (level[owner_of][None, :] * 256 + noise + (owner_of == hottest).astype(jnp.int32)[None, :] * 4096) * slots + index[None, :]
    top_values, chosen = lax.top_k(score, ROW_DEV)
    order_key = jax.random.randint(jax.random.fold_in(key, 23), (devices, ROW_DEV), 0, 1 << 20) * ROW_DEV + jnp.arange(ROW_DEV, dtype=jnp.int32)[None, :]
    order = jnp.argsort(order_key, axis=1, stable=True)
    chosen = jnp.take_along_axis(chosen, order, axis=1).reshape(ROWS).astype(jnp.int32)
    owner = chosen // CAP
    local = jax.random.randint(jax.random.fold_in(key, 24), (ROWS,), 0, CL_DEV)
    return ((owner * CL_DEV + local).astype(jnp.int32), (chosen % CAP).astype(jnp.int32))


def draw_cluster(key, part):
    return route_table(key)[0]


def draw_slot(key, part):
    return route_table(key)[1]


def setup_inputs(seed: int = 0) -> dict:
    seeds = jax.random.split(jax.random.key(seed), 5)
    return {
        "embeddings": draw_embeddings(jax.random.fold_in(seeds[4], 71), 0),
        "centroids": draw_centroids(jax.random.fold_in(seeds[4], 71), 0),
        "cluster": draw_cluster(jax.random.fold_in(seeds[4], 71), 0),
        "slot": draw_slot(jax.random.fold_in(seeds[4], 71), 0),
    }


inverse_temp = 256.0

def unit_rows(values):
    total = lax.optimization_barrier(jnp.sum(values * values, axis=1, keepdims=True))
    return (values * lax.rsqrt(total + 1e-06)).astype(jnp.bfloat16)

def inner_rows(left, right):
    return lax.dot_general(left, right, (((1,), (1,)), ((), ())), preferred_element_type=jnp.float32)

def owner_best(rows, ids):
    total = rows.shape[0]
    block = min(512, total)
    col_pos = jnp.arange(total)

    def one_block(index):
        start = index * block
        part = lax.dynamic_slice_in_dim(rows, start, block, 0)
        part_ids = lax.dynamic_slice_in_dim(ids, start, block, 0)
        gram = inner_rows(part, rows)
        row_pos = start + jnp.arange(block)
        mask = (part_ids[:, None] == ids[None, :]) & (ids[None, :] >= 0.0) & (col_pos[None, :] < row_pos[:, None])
        return lax.optimization_barrier(jnp.max(jnp.where(mask, gram, jnp.float32(-1.0)), axis=1))
    return lax.map(one_block, jnp.arange(total // block)).reshape(total)

def reference(embeddings, centroids, cluster, slot):
    devices = N_DOC * N_CENT
    unit = unit_rows(embeddings)
    centre = unit_rows(centroids)

    def cost_block(part):
        score = inner_rows(part, centre) * inverse_temp
        high = lax.optimization_barrier(jnp.max(score, axis=1))
        total = lax.optimization_barrier(jnp.sum(jnp.exp(score - high[:, None]), axis=1))
        return 1.0 - (high + jnp.log(total)) / inverse_temp
    soft_cost = lax.map(cost_block, unit.reshape(devices, ROW_DEV, D)).reshape(ROWS)
    owner = cluster // CL_DEV
    local = (cluster % CL_DEV).astype(jnp.float32)
    source = (jnp.arange(ROWS) // ROW_DEV).astype(jnp.int32)
    place = (owner * (devices * CAP) + source * CAP + slot).astype(jnp.int32)
    every_row = jnp.zeros((devices * devices * CAP, D), jnp.bfloat16).at[place].set(unit)
    every_id = jnp.full((devices * devices * CAP,), -1.0, jnp.float32).at[place].set(local)
    best = lax.map(lambda pair: owner_best(pair[0], pair[1]), (every_row.reshape(devices, devices * CAP, D), every_id.reshape(devices, devices * CAP)))
    dup_sim = best.reshape(-1)[place]
    return (soft_cost, dup_sim)
```

```python
import functools
import math

import jax
import jax.numpy as jnp
from jax import lax
from jax.experimental import pallas as pl
from jax.experimental.pallas import tpu as pltpu
from jax.sharding import PartitionSpec as P

INVERSE_TEMP = 256.0
SCALE = INVERSE_TEMP / math.log(2.0)
BACK = math.log(2.0) / INVERSE_TEMP
NT = (((1,), (1,)), ((), ()))
ID_LANES = 128
VMEM = pl.BlockSpec(memory_space=pltpu.VMEM)
LIMIT = 48 * 1024 * 1024


def params():
    return pltpu.CompilerParams(vmem_limit_bytes=LIMIT)


def unit_of(values):
    total = jnp.sum(values * values, axis=1, keepdims=True)
    return (values * lax.rsqrt(total + 1e-06)).astype(jnp.bfloat16)


def target_row(cluster, slot, per_owner, cap):
    return (cluster // per_owner) * cap + slot


def rows_kernel(per_owner, cap, emb_ref, cluster_ref, slot_ref, low_ref, high_ref, send_ref):
    unit = unit_of(emb_ref[...])
    half = unit.shape[0] // 2
    low_ref[...] = unit[:half]
    high_ref[...] = unit[half:]
    cluster = cluster_ref[...]
    target = target_row(cluster, slot_ref[...], per_owner, cap)
    local = (cluster % per_owner + 1).astype(jnp.float32)
    ids = jnp.broadcast_to(local, (ID_LANES, local.shape[1])).astype(jnp.bfloat16)
    total = send_ref.shape[0]
    width = unit.shape[1]
    block = 256
    for start in range(0, total, block):
        place = start + lax.broadcasted_iota(jnp.int32, (block, unit.shape[0]), 0)
        hot = (place == target).astype(jnp.float32).astype(jnp.bfloat16)
        send_ref[start : start + block, :width] = lax.dot_general(
            hot, unit, (((1,), (0,)), ((), ())), preferred_element_type=jnp.float32
        ).astype(jnp.bfloat16)
        send_ref[start : start + block, width:] = (
            lax.dot_general(hot, ids, NT, preferred_element_type=jnp.float32) - 1.0
        ).astype(jnp.bfloat16)


def prepare_rows(embeddings, cluster, slot, per_owner, cap, devices):
    rows, width = embeddings.shape
    half = jax.ShapeDtypeStruct((rows // 2, width), jnp.bfloat16)
    return pl.pallas_call(
        functools.partial(rows_kernel, per_owner, cap),
        out_shape=(
            half,
            half,
            jax.ShapeDtypeStruct((devices * cap, width + ID_LANES), jnp.bfloat16),
        ),
        in_specs=[VMEM] * 3,
        out_specs=(VMEM,) * 3,
        compiler_params=params(),
        cost_estimate=pl.CostEstimate(
            flops=2 * devices * cap * rows * width, bytes_accessed=6 * rows * width, transcendentals=0
        ),
        name="prepare_rows",
    )(embeddings, cluster.reshape(1, rows), slot.reshape(1, rows))


def centre_kernel(cen_ref, low_ref, high_ref):
    @pl.when(pl.program_id(0) < 2)
    def _():
        low_ref[...] = unit_of(cen_ref[...])

    @pl.when(pl.program_id(0) >= 2)
    def _():
        high_ref[...] = unit_of(cen_ref[...])


def prepare_centres(centroids):
    count, width = centroids.shape
    half = jax.ShapeDtypeStruct((count // 2, width), jnp.bfloat16)
    block = count // 4
    return pl.pallas_call(
        centre_kernel,
        grid=(4,),
        out_shape=(half, half),
        in_specs=[pl.BlockSpec((block, width), lambda i: (i, 0))],
        out_specs=(
            pl.BlockSpec((block, width), lambda i: (jnp.minimum(i, 1), 0)),
            pl.BlockSpec((block, width), lambda i: (jnp.maximum(i - 2, 0), 0)),
        ),
        compiler_params=params(),
        cost_estimate=pl.CostEstimate(
            flops=4 * count * width, bytes_accessed=6 * count * width, transcendentals=count
        ),
        name="prepare_centres",
    )(centroids)


def score_kernel(n_rows, n_cent, step, *refs):
    row_refs = refs[:n_rows]
    cent_refs = refs[n_rows : n_rows + n_cent]
    out_ref = refs[n_rows + n_cent]
    table, high, total, sems = refs[n_rows + n_cent + 1 :]
    part = cent_refs[0].shape[0]
    block = row_refs[0].shape[0]
    copies = [
        pltpu.make_async_copy(ref, table.at[pl.ds(i * part, part)], sems.at[i])
        for i, ref in enumerate(cent_refs)
    ]
    for copy in copies:
        copy.start()
    high[...] = jnp.full_like(high, -1e30)
    total[...] = jnp.zeros_like(total)
    for i in range(n_cent):
        copies[i].wait()

        @pl.loop(0, part // step)
        def _(k):
            start = pl.multiple_of(i * part + k * step, step)
            centre = table[pl.ds(start, step), :]
            for j in range(n_rows):
                lanes = slice(j * block, (j + 1) * block)
                score = SCALE * lax.dot_general(
                    centre, row_refs[j][...], NT, preferred_element_type=jnp.float32
                )
                score = score.reshape(step // 8, 8, block)
                before = high[:, lanes]
                now = jnp.maximum(before, jnp.max(score, axis=0))
                high[:, lanes] = now
                total[:, lanes] = total[:, lanes] * jnp.exp2(before - now) + jnp.sum(
                    jnp.exp2(score - now[None]), axis=0
                )

    top = jnp.max(high[...], axis=0, keepdims=True)
    all_sum = jnp.sum(total[...] * jnp.exp2(high[...] - top), axis=0, keepdims=True)
    out_ref[...] = top + jnp.log2(all_sum)


def score(rows, centres, name):
    block, width = rows[0].shape
    part = centres[0].shape[0]
    count = len(rows) * block
    table = len(centres) * part
    return pl.pallas_call(
        functools.partial(score_kernel, len(rows), len(centres), 256),
        out_shape=jax.ShapeDtypeStruct((1, count), jnp.float32),
        in_specs=[VMEM] * len(rows) + [pl.BlockSpec(memory_space=pl.ANY)] * len(centres),
        out_specs=VMEM,
        scratch_shapes=[
            pltpu.VMEM((table, width), jnp.bfloat16),
            pltpu.VMEM((8, count), jnp.float32),
            pltpu.VMEM((8, count), jnp.float32),
            pltpu.SemaphoreType.DMA((len(centres),)),
        ],
        compiler_params=params(),
        cost_estimate=pl.CostEstimate(
            flops=2 * count * table * width,
            bytes_accessed=2 * (count + table) * width,
            transcendentals=count * table,
        ),
        name=name,
    )(*rows, *centres)


def owner_kernel(rows_ref, out_ref):
    total = rows_ref.shape[0]
    width = rows_ref.shape[1] - ID_LANES
    block = 256
    pick = (lax.broadcasted_iota(jnp.int32, (8, ID_LANES), 1) == 0).astype(jnp.float32)
    pick = pick.astype(jnp.bfloat16)
    ids = rows_ref[:, width:]
    id_row = lax.dot_general(pick, ids, NT, preferred_element_type=jnp.float32)[:1]
    for col in range(0, total, block):
        best = jnp.full((8, block), -1.0, jnp.float32)
        for row in range(0, col + block, block):
            gram = lax.dot_general(
                rows_ref[row : row + block, :width],
                rows_ref[col : col + block, :width],
                NT,
                preferred_element_type=jnp.float32,
            )
            id_col = ids[row : row + block].astype(jnp.float32)
            id_col = jnp.concatenate([id_col] * (block // ID_LANES), axis=1)
            same = id_col == id_row[:, col : col + block]
            if row == col:
                s = lax.broadcasted_iota(jnp.int32, (block, block), 0)
                r = lax.broadcasted_iota(jnp.int32, (block, block), 1)
                same = same & (s < r)
            gram = jnp.where(same, gram, -1.0).reshape(block // 8, 8, block)
            best = jnp.maximum(best, jnp.max(gram, axis=0))
        out_ref[:, col : col + block] = jnp.max(best, axis=0, keepdims=True)


def owner_best(rows):
    total, width = rows.shape
    return pl.pallas_call(
        owner_kernel,
        out_shape=jax.ShapeDtypeStruct((1, total), jnp.float32),
        in_specs=[VMEM],
        out_specs=VMEM,
        compiler_params=params(),
        cost_estimate=pl.CostEstimate(
            flops=2 * total * total * width, bytes_accessed=2 * total * width, transcendentals=0
        ),
        name="owner_best",
    )(rows)


def pick_kernel(per_owner, got_ref, cluster_ref, slot_ref, out_ref):
    got = got_ref[...]
    devices, cap = got.shape
    rows = out_ref.shape[1]
    owner = cluster_ref[...] // per_owner
    hot = (lax.broadcasted_iota(jnp.int32, (devices, rows), 0) == owner).astype(jnp.float32)
    by_slot = lax.dot_general(
        got,
        hot,
        (((0,), (0,)), ((), ())),
        precision=lax.Precision.HIGHEST,
        preferred_element_type=jnp.float32,
    )
    mine = lax.broadcasted_iota(jnp.int32, (cap, rows), 0) == slot_ref[...]
    out_ref[...] = jnp.sum(jnp.where(mine, by_slot, 0.0), axis=0, keepdims=True)


def pick(got, cluster, slot, per_owner):
    rows = cluster.shape[0]
    return pl.pallas_call(
        functools.partial(pick_kernel, per_owner),
        out_shape=jax.ShapeDtypeStruct((1, rows), jnp.float32),
        in_specs=[VMEM] * 3,
        out_specs=VMEM,
        compiler_params=params(),
        cost_estimate=pl.CostEstimate(
            flops=16 * got.shape[0] * rows, bytes_accessed=32 * rows, transcendentals=0
        ),
        name="pick",
    )(got, cluster.reshape(1, rows), slot.reshape(1, rows)).reshape(rows)


def moves(step):
    pairs = []
    for y in range(4):
        for x in range(4):
            for z in range(4):
                for core in range(2):
                    here, there = [
                        (b * 2 + a // 2) * 16 + (c * 2 + a % 2) * 2 + d
                        for a, b, c, d in ((x, y, z, core), step(x, y, z, core))
                    ]
                    pairs.append((here, there))
    return pairs


def move_x(value, by):
    return lax.ppermute(
        value, ("doc", "cent"), moves(lambda x, y, z, core: ((x + by) % 4, y, z, core))
    )


def move_z(value, by):
    return lax.ppermute(value, ("doc", "cent"), moves(lambda x, y, z, core: (x, y, (z + by) % 4, core)))


def swap_core(value):
    return lax.ppermute(value, ("doc", "cent"), moves(lambda x, y, z, core: (x, y, z, 1 - core)))


def per_device(embeddings, centroids, cluster, slot):
    row_count, width = embeddings.shape
    devices = lax.axis_size("doc") * lax.axis_size("cent")
    per_owner = centroids.shape[0] // lax.axis_size("doc")
    cap = 2 * row_count // devices

    low, high, send = prepare_rows(embeddings, cluster, slot, per_owner, cap, devices)
    low_up, high_down = move_z(low, 1), move_z(high, -1)
    high_up, low_down = move_z(high, 1), move_z(low, -1)
    low_far, high_far = move_z(low_up, 1), move_z(high_down, -1)

    got = lax.all_to_all(
        send.reshape(devices, cap, width + ID_LANES),
        ("doc", "cent"),
        split_axis=0,
        concat_axis=0,
        tiled=True,
    )

    centre_low, centre_high = prepare_centres(centroids)
    side_low, side_high = move_x(centre_low, 1), move_x(centre_high, -1)
    core_low, core_high = swap_core(centre_low), swap_core(centre_high)
    side_core_low, side_core_high = swap_core(side_low), swap_core(side_high)
    centres = (
        centre_low,
        centre_high,
        core_low,
        core_high,
        side_low,
        side_high,
        side_core_low,
        side_core_high,
    )

    near = score((low, high, low_up, high_up, low_down, high_down), centres, "score_near")
    mine, below, above = [near[:, i * row_count : (i + 1) * row_count] for i in range(3)]
    far = score((low_far, high_far), centres, "score_far")

    best = owner_best(got.reshape(devices * cap, width + ID_LANES))
    returned = lax.all_to_all(
        best.reshape(devices, cap), ("doc", "cent"), split_axis=0, concat_axis=0, tiled=True
    )
    dup_sim = pick(returned, cluster, slot, per_owner)

    terms = jnp.concatenate([mine, move_z(below, -1), move_z(above, 1), move_z(far, 2)], axis=0)
    top = jnp.max(terms, axis=0)
    soft_cost = 1.0 - BACK * (top + jnp.log2(jnp.sum(jnp.exp2(terms - top[None]), axis=0)))
    return (soft_cost, dup_sim)


def solution(mesh):
    return jax.shard_map(
        per_device,
        mesh=mesh,
        in_specs=(
            P(("doc", "cent"), None),
            P("cent", None),
            P(("doc", "cent")),
            P(("doc", "cent")),
        ),
        out_specs=(P(("doc", "cent")), P(("doc", "cent"))),
        check_vma=False,
    )
```

```python
import functools
import math

import jax
import jax.numpy as jnp
from jax import lax
from jax.experimental import pallas as pl
from jax.experimental.pallas import tpu as pltpu
from jax.sharding import PartitionSpec as P

INVERSE_TEMP = 256.0
SCALE = INVERSE_TEMP / math.log(2.0)
BACK = math.log(2.0) / INVERSE_TEMP
NT = (((1,), (1,)), ((), ()))
ID_LANES = 128
LANES = 256
VMEM = pl.BlockSpec(memory_space=pltpu.VMEM)
TINY = pl.CostEstimate(flops=1, bytes_accessed=1, transcendentals=0)


PARAMS = pltpu.CompilerParams(vmem_limit_bytes=60 * 1024 * 1024)
SCORE_PARAMS = pltpu.CompilerParams(vmem_limit_bytes=24 * 1024 * 1024)
ANY = pl.BlockSpec(memory_space=pl.ANY)
CHUNK = 128
STEP = 512


def unit_of(values):
    total = jnp.sum(values * values, axis=1, keepdims=True)
    return (values * lax.rsqrt(total + 1e-06)).astype(jnp.bfloat16)


def prepare_kernel(per_owner, cap, *refs):
    emb_hbm, cen_hbm, cluster_hbm, slot_hbm = refs[:4]
    unit_hbm, send_hbm, centre_hbm = refs[4:7]
    emb, cen, cluster_ref, slot_ref, unit_ref, send_ref, centre_ref = refs[7:14]
    emb_sems, cen_sems, id_sems, unit_sems, send_sems, centre_sems = refs[14:]
    rows, width = emb.shape

    def copy_of(src, dst, sem):
        return pltpu.make_async_copy(src, dst, sem)

    def piece(ref, i, size=CHUNK):
        return ref.at[pl.ds(i * size, size)]

    ids = [
        copy_of(cluster_hbm, cluster_ref, id_sems.at[0]),
        copy_of(slot_hbm, slot_ref, id_sems.at[1]),
    ]
    emb_copies = [
        copy_of(piece(emb_hbm, i), piece(emb, i), emb_sems.at[i]) for i in range(rows // CHUNK)
    ]
    cen_copies = [
        copy_of(piece(cen_hbm, i), piece(cen, i), cen_sems.at[i])
        for i in range(cen.shape[0] // CHUNK)
    ]
    for copy in emb_copies + ids + cen_copies:
        copy.start()
    out = []

    def send_out(src, dst, sem):
        out.append(copy_of(src, dst, sem))
        out[-1].start()

    for i, copy in enumerate(emb_copies):
        copy.wait()
        part = slice(i * CHUNK, (i + 1) * CHUNK)
        unit_ref[part] = unit_of(emb[part])
        send_out(piece(unit_ref, i), piece(unit_hbm, i), unit_sems.at[i])
    for copy in ids:
        copy.wait()
    cluster = cluster_ref[...]
    target = (cluster // per_owner) * cap + slot_ref[...]
    local = (cluster % per_owner + 1).astype(jnp.float32)
    names = jnp.broadcast_to(local, (ID_LANES, rows)).astype(jnp.bfloat16)
    for i in range(send_ref.shape[0] // LANES):
        part = slice(i * LANES, (i + 1) * LANES)
        place = i * LANES + lax.broadcasted_iota(jnp.int32, (LANES, rows), 0)
        hot = (place == target).astype(jnp.float32).astype(jnp.bfloat16)
        send_ref[part, :width] = lax.dot_general(
            hot, unit_ref[...], (((1,), (0,)), ((), ())), preferred_element_type=jnp.float32
        ).astype(jnp.bfloat16)
        send_ref[part, width:] = (
            lax.dot_general(hot, names, NT, preferred_element_type=jnp.float32) - 1.0
        ).astype(jnp.bfloat16)
        send_out(piece(send_ref, i, LANES), piece(send_hbm, i, LANES), send_sems.at[i])
    for i, copy in enumerate(cen_copies):
        copy.wait()
        part = slice(i * CHUNK, (i + 1) * CHUNK)
        centre_ref[part] = unit_of(cen[part])
        send_out(piece(centre_ref, i), piece(centre_hbm, i), centre_sems.at[i])
    for copy in out:
        copy.wait()


def prepare(embeddings, centroids, cluster, slot, per_owner, cap, devices):
    rows, width = embeddings.shape
    count = centroids.shape[0]
    send = (devices * cap, width + ID_LANES)
    shapes = ((rows, width), send, (count, width))
    sems = (rows // CHUNK, count // CHUNK, 2, rows // CHUNK, send[0] // LANES)
    sems += (count // CHUNK,)
    return pl.pallas_call(
        functools.partial(prepare_kernel, per_owner, cap),
        out_shape=tuple(jax.ShapeDtypeStruct(shape, jnp.bfloat16) for shape in shapes),
        in_specs=[ANY] * 4,
        out_specs=(ANY,) * 3,
        scratch_shapes=[
            pltpu.VMEM((rows, width), jnp.float32),
            pltpu.VMEM((count, width), jnp.float32),
            pltpu.VMEM((1, rows), jnp.int32),
            pltpu.VMEM((1, rows), jnp.int32),
            pltpu.VMEM((rows, width), jnp.bfloat16),
            pltpu.VMEM(send, jnp.bfloat16),
            pltpu.VMEM((count, width), jnp.bfloat16),
        ]
        + [pltpu.SemaphoreType.DMA((n,)) for n in sems],
        compiler_params=PARAMS,
        cost_estimate=TINY,
        name="prepare",
    )(embeddings, centroids, cluster.reshape(1, rows), slot.reshape(1, rows))


def score_kernel(n_rows, sizes, fetch, plan, *refs):
    n_cent = len(sizes)
    row_refs, refs = refs[:n_rows], refs[n_rows:]
    if fetch:
        cent_refs, (out_ref, table), refs = refs[:n_cent], refs[n_cent : n_cent + 2], refs[n_cent + 2 :]
    else:
        cent_refs, (table, out_ref), refs = (), refs[:2], refs[2:]
    rows, high, total, row_sems, cent_sems = refs

    def copies_of(arrays, buffer, sems):
        copies, i, base = [], 0, 0
        for ref in arrays:
            mine = []
            size = min(STEP, ref.shape[0])
            for start in range(0, ref.shape[0], size):
                mine.append(
                    pltpu.make_async_copy(
                        ref.at[pl.ds(start, size)], buffer.at[pl.ds(base + start, size)], sems.at[i]
                    )
                )
                i += 1
            copies.append(mine)
            base += ref.shape[0]
        return copies

    row_starts = [sum(ref.shape[0] for ref in row_refs[:j]) for j in range(n_rows)]
    cent_starts = [sum(sizes[:i]) for i in range(n_cent)]
    row_copies = copies_of(row_refs, rows, row_sems)
    cent_copies = copies_of(cent_refs, table, cent_sems)
    stages = [
        [copy for j in new_rows for copy in row_copies[j]]
        + [copy for i in new_cents if fetch for copy in cent_copies[i]]
        for new_rows, new_cents, _ in plan
    ]

    def product(cent, lanes):
        return lax.dot_general(
            table[pl.ds(cent, STEP)], rows[lanes], NT, preferred_element_type=jnp.float32
        )

    for copy in stages[0]:
        copy.start()
    begun = set()
    for k, (_, _, products) in enumerate(plan):
        for copy in stages[k]:
            copy.wait()
        for copy in stages[k + 1] if k + 1 < len(plan) else []:
            copy.start()
        for i, j in products:
            for row in range(row_starts[j], row_starts[j] + row_refs[j].shape[0], LANES):
                lanes = slice(row, row + LANES)
                for cent in range(cent_starts[i], cent_starts[i] + sizes[i], STEP):
                    value = product(cent, lanes) * SCALE
                    if row not in begun:
                        shift = jnp.max(value, axis=0, keepdims=True)
                        high[:, lanes] = jnp.broadcast_to(shift, (8, LANES))
                    value = jnp.exp2(value.reshape(STEP // 8, 8, LANES) - high[:, lanes][None])
                    value = jnp.sum(value, axis=0)
                    total[:, lanes] = value if row not in begun else total[:, lanes] + value
                    begun.add(row)

    @pl.when(jnp.logical_not(jnp.max(total[...]) < 1e38))
    def _():
        high[...] = jnp.full_like(high, -1e30)
        total[...] = jnp.zeros_like(total)
        for i, j in [pair for _, _, products in plan for pair in products]:

            @pl.loop(0, row_refs[j].shape[0] // LANES)
            def _(r):
                @pl.loop(0, sizes[i] // STEP)
                def _(c):
                    lanes = pl.ds(pl.multiple_of(row_starts[j] + r * LANES, LANES), LANES)
                    value = product(pl.multiple_of(cent_starts[i] + c * STEP, STEP), lanes) * SCALE
                    value = value.reshape(STEP // 8, 8, LANES)
                    before = high[:, lanes]
                    now = jnp.maximum(before, jnp.max(value, axis=0))
                    high[:, lanes] = now
                    total[:, lanes] = total[:, lanes] * jnp.exp2(before - now) + jnp.sum(
                        jnp.exp2(value - now[None]), axis=0
                    )

    top = jnp.max(high[...], axis=0, keepdims=True)
    all_sum = jnp.sum(total[...] * jnp.exp2(high[...] - top), axis=0, keepdims=True)
    out_ref[...] = top + jnp.log2(all_sum)


def score(rows, centres, plan, name, sizes=None):
    fetch = sizes is None
    if fetch:
        sizes = tuple(value.shape[0] for value in centres)
    width = rows[0].shape[1]
    count = sum(value.shape[0] for value in rows)
    out = jax.ShapeDtypeStruct((1, count), jnp.float32)
    table = jax.ShapeDtypeStruct((sum(sizes), width), jnp.bfloat16)
    return pl.pallas_call(
        functools.partial(score_kernel, len(rows), sizes, fetch, plan),
        out_shape=(out, table) if fetch else out,
        in_specs=[ANY] * len(rows) + ([ANY] * len(centres) if fetch else [VMEM]),
        out_specs=(VMEM, VMEM) if fetch else VMEM,
        scratch_shapes=[
            pltpu.VMEM((count, width), jnp.bfloat16),
            pltpu.VMEM((8, count), jnp.float32),
            pltpu.VMEM((8, count), jnp.float32),
            pltpu.SemaphoreType.DMA((count // LANES,)),
            pltpu.SemaphoreType.DMA((sum(sizes) // STEP,)),
        ],
        compiler_params=SCORE_PARAMS,
        cost_estimate=TINY,
        name=name,
    )(*rows, *(centres if fetch else (centres,)))


def owner_kernel(rows_hbm, out_ref, rows_ref, sems):
    total = rows_ref.shape[0]
    width = rows_ref.shape[1] - ID_LANES
    cap = out_ref.shape[1]
    block = LANES
    copies = [
        pltpu.make_async_copy(
            rows_hbm.at[pl.ds(i * block, block)], rows_ref.at[pl.ds(i * block, block)], sems.at[i]
        )
        for i in range(total // block)
    ]
    for copy in copies:
        copy.start()
    pick = (lax.broadcasted_iota(jnp.int32, (8, ID_LANES), 1) == 0).astype(jnp.float32)
    pick = pick.astype(jnp.bfloat16)
    r = lax.broadcasted_iota(jnp.int32, (block, block), 0)
    s = lax.broadcasted_iota(jnp.int32, (block, block), 1)
    eye = lax.broadcasted_iota(jnp.int32, (cap, ID_LANES), 0)
    eye = (eye == lax.broadcasted_iota(jnp.int32, (cap, ID_LANES), 1)).astype(jnp.float32)
    id_rows = []
    for row in range(0, total, block):
        if row in (0, total // 2):
            for copy in copies[row // block : (row + total // 2) // block]:
                copy.wait()
        ids = rows_ref[row : row + block, width:]
        id_rows.append(lax.dot_general(pick, ids, NT, preferred_element_type=jnp.float32)[:1])
        id_col = ids.astype(jnp.float32)
        best = jnp.full((block, ID_LANES), -1.0, jnp.float32)
        for col in range(0, row + block, block):
            gram = lax.dot_general(
                rows_ref[row : row + block, :width],
                rows_ref[col : col + block, :width],
                NT,
                preferred_element_type=jnp.float32,
            )
            for lane in range(0, block, ID_LANES):
                lanes = slice(lane, lane + ID_LANES)
                same = id_col == id_rows[col // block][:, lanes]
                if row == col:
                    same = same & (s < r)[:, lanes]
                best = jnp.maximum(best, jnp.where(same, gram[:, lanes], -1.0))
        best = jnp.max(best, axis=1, keepdims=True).reshape(block // cap, cap, 1)
        best = jnp.sum(best * eye[None], axis=1)
        out_ref[row // cap : (row + block) // cap, :] = best[:, :cap]


def owner_best(rows, cap):
    total, width = rows.shape
    return pl.pallas_call(
        owner_kernel,
        out_shape=jax.ShapeDtypeStruct((total // cap, cap), jnp.float32),
        in_specs=[ANY],
        out_specs=VMEM,
        scratch_shapes=[
            pltpu.VMEM((total, width), jnp.bfloat16),
            pltpu.SemaphoreType.DMA((total // LANES,)),
        ],
        compiler_params=SCORE_PARAMS,
        cost_estimate=TINY,
        name="owner_best",
    )(rows)


def pick_kernel(per_owner, got_ref, cluster_ref, slot_ref, out_ref):
    got = got_ref[...]
    devices, cap = got.shape
    rows = out_ref.shape[1]
    owner = cluster_ref[...] // per_owner
    hot = (lax.broadcasted_iota(jnp.int32, (devices, rows), 0) == owner).astype(jnp.float32)
    by_slot = lax.dot_general(
        got,
        hot,
        (((0,), (0,)), ((), ())),
        precision=lax.Precision.HIGHEST,
        preferred_element_type=jnp.float32,
    )
    mine = lax.broadcasted_iota(jnp.int32, (cap, rows), 0) == slot_ref[...]
    out_ref[...] = jnp.sum(jnp.where(mine, by_slot, 0.0), axis=0, keepdims=True)


def pick(got, cluster, slot, per_owner):
    rows = cluster.shape[0]
    return pl.pallas_call(
        functools.partial(pick_kernel, per_owner),
        out_shape=jax.ShapeDtypeStruct((1, rows), jnp.float32),
        in_specs=[VMEM] * 3,
        out_specs=VMEM,
        compiler_params=SCORE_PARAMS,
        cost_estimate=TINY,
        name="pick",
    )(got, cluster.reshape(1, rows), slot.reshape(1, rows)).reshape(rows)


def move(value, step):
    pairs = []
    for y in range(4):
        for x in range(4):
            for z in range(4):
                for core in range(2):
                    here, there = [
                        (y * 2 + a % 4 // 2) * 16 + (b % 4 * 2 + a % 2) * 2 + c
                        for a, b, c in ((x, z, core), step(x, z, core))
                    ]
                    pairs.append((here, there))
    return lax.ppermute(value, ("doc", "cent"), pairs)


def swap_core(value):
    return move(value, lambda x, z, core: (x, z, 1 - core))


def move_x(value):
    return move(value, lambda x, z, core: (x + 1 - 2 * core, z, core))


def move_z(value, by):
    return move(value, lambda x, z, core: (x, z + by * (1 - 2 * core), core))


def per_device(embeddings, centroids, cluster, slot):
    row_count, width = embeddings.shape
    devices = lax.axis_size("doc") * lax.axis_size("cent")
    per_owner = centroids.shape[0] // lax.axis_size("doc")
    cap = 2 * row_count // devices

    unit, send, centre = prepare(embeddings, centroids, cluster, slot, per_owner, cap, devices)
    ahead, behind = move_z(unit, 1), move_z(unit, -1)
    side, core = move_x(centre), swap_core(centre)
    plan = (((0,), (0,), ((0, 0),)), ((), (1,), ((1, 0),)))
    first, _ = score((unit,), (centre, core), plan, "score_own")

    def after(value, done):
        return lax.optimization_barrier((value, done))[0]

    got = lax.all_to_all(
        send.reshape(devices, cap, width + ID_LANES),
        ("doc", "cent"),
        split_axis=0,
        concat_axis=0,
        tiled=True,
    )
    side, ahead, behind = after(side, first), after(ahead, first), after(behind, first)
    side_core = swap_core(after(side, (ahead, behind)))
    far = move_z(ahead, 1)
    best = owner_best(after(got, first).reshape(devices * cap, width + ID_LANES), cap)
    returned = lax.all_to_all(best, ("doc", "cent"), split_axis=0, concat_axis=0, tiled=True)

    centres = (side, side_core, centre, core)
    plan = (
        ((0, 1), (0,), ((0, 0), (0, 1))),
        ((2,), (1,), ((1, 0), (1, 1), (0, 2), (1, 2))),
        ((), (2, 3), ((2, 1), (2, 2), (3, 1), (3, 2))),
    )
    near, table = score((unit, ahead, after(behind, best)), centres, plan, "score_near")
    parts = [near[:, i * row_count : (i + 1) * row_count] for i in range(3)]
    plan = (((0,), (0, 1, 2, 3), ((0, 0), (1, 0), (2, 0), (3, 0))),)
    sizes = tuple(value.shape[0] for value in centres)
    last = score((far,), table, plan, "score_far", sizes)

    terms = (first, parts[0], move_z(parts[1], -1), move_z(parts[2], 1))
    terms = jnp.concatenate([*terms, move_z(last, 2)], axis=0)
    top = jnp.max(terms, axis=0)
    soft_cost = 1.0 - BACK * (top + jnp.log2(jnp.sum(jnp.exp2(terms - top[None]), axis=0)))
    dup_sim = pick(returned, cluster, slot, per_owner)
    return (soft_cost, dup_sim)


def solution(mesh):
    return jax.shard_map(
        per_device,
        mesh=mesh,
        in_specs=(
            P(("doc", "cent"), None),
            P("cent", None),
            P(("doc", "cent")),
            P(("doc", "cent")),
        ),
        out_specs=(P(("doc", "cent")), P(("doc", "cent"))),
        check_vma=False,
    )
```

```python
import functools
import math

import jax
import jax.numpy as jnp
from jax import lax
from jax.experimental import pallas as pl
from jax.experimental.pallas import tpu as pltpu
from jax.sharding import PartitionSpec as P

INVERSE_TEMP = 256.0
SCALE = INVERSE_TEMP / math.log(2.0)
BACK = math.log(2.0) / INVERSE_TEMP
NT = (((1,), (1,)), ((), ()))
ID_LANES = 128
LANES = 256
VMEM = pl.BlockSpec(memory_space=pltpu.VMEM)
TINY = pl.CostEstimate(flops=1, bytes_accessed=1, transcendentals=0)


PARAMS = pltpu.CompilerParams(vmem_limit_bytes=60 * 1024 * 1024)
SCORE_PARAMS = pltpu.CompilerParams(vmem_limit_bytes=24 * 1024 * 1024)
ANY = pl.BlockSpec(memory_space=pl.ANY)
CHUNK = 128
STEP = 512


def in_hbm(value):
    return pltpu.with_memory_space_constraint(value, pltpu.HBM)


def unit_of(values):
    total = jnp.sum(values * values, axis=1, keepdims=True)
    return (values * lax.rsqrt(total + 1e-06)).astype(jnp.bfloat16)


def rows_kernel(per_owner, cap, *refs):
    emb_hbm, cluster_hbm, slot_hbm, unit_hbm, send_hbm = refs[:5]
    emb, cluster_ref, slot_ref, unit_ref, send_ref = refs[5:10]
    emb_sems, id_sems, unit_sems, send_sems = refs[10:]
    rows, width = emb.shape

    def piece(ref, i, size=CHUNK):
        return ref.at[pl.ds(i * size, size)]

    ids = [
        pltpu.make_async_copy(cluster_hbm, cluster_ref, id_sems.at[0]),
        pltpu.make_async_copy(slot_hbm, slot_ref, id_sems.at[1]),
    ]
    emb_copies = [
        pltpu.make_async_copy(piece(emb_hbm, i), piece(emb, i), emb_sems.at[i])
        for i in range(rows // CHUNK)
    ]
    for copy in emb_copies + ids:
        copy.start()
    out = []

    def send_out(src, dst, sem):
        out.append(pltpu.make_async_copy(src, dst, sem))
        out[-1].start()

    for i, copy in enumerate(emb_copies):
        copy.wait()
        part = slice(i * CHUNK, (i + 1) * CHUNK)
        unit_ref[part] = unit_of(emb[part])
        send_out(piece(unit_ref, i), piece(unit_hbm, i), unit_sems.at[i])
    for copy in ids:
        copy.wait()
    cluster = cluster_ref[...]
    target = (cluster // per_owner) * cap + slot_ref[...]
    local = (cluster % per_owner + 1).astype(jnp.float32)
    names = jnp.broadcast_to(local, (ID_LANES, rows)).astype(jnp.bfloat16)
    for i in range(send_ref.shape[0] // LANES):
        part = slice(i * LANES, (i + 1) * LANES)
        place = i * LANES + lax.broadcasted_iota(jnp.int32, (LANES, rows), 0)
        hot = (place == target).astype(jnp.float32).astype(jnp.bfloat16)
        send_ref[part, :width] = lax.dot_general(
            hot, unit_ref[...], (((1,), (0,)), ((), ())), preferred_element_type=jnp.float32
        ).astype(jnp.bfloat16)
        send_ref[part, width:] = (
            lax.dot_general(hot, names, NT, preferred_element_type=jnp.float32) - 1.0
        ).astype(jnp.bfloat16)
        send_out(piece(send_ref, i, LANES), piece(send_hbm, i, LANES), send_sems.at[i])
    for copy in out:
        copy.wait()


def prepare_rows(embeddings, cluster, slot, per_owner, cap, devices):
    rows, width = embeddings.shape
    send = (devices * cap, width + ID_LANES)
    return pl.pallas_call(
        functools.partial(rows_kernel, per_owner, cap),
        out_shape=tuple(jax.ShapeDtypeStruct(shape, jnp.bfloat16) for shape in ((rows, width), send)),
        in_specs=[ANY] * 3,
        out_specs=(ANY,) * 2,
        scratch_shapes=[
            pltpu.VMEM((rows, width), jnp.float32),
            pltpu.VMEM((1, rows), jnp.int32),
            pltpu.VMEM((1, rows), jnp.int32),
            pltpu.VMEM((rows, width), jnp.bfloat16),
            pltpu.VMEM(send, jnp.bfloat16),
        ]
        + [pltpu.SemaphoreType.DMA((n,)) for n in (rows // CHUNK, 2, rows // CHUNK, send[0] // LANES)],
        compiler_params=PARAMS,
        cost_estimate=TINY,
        name="prepare_rows",
    )(embeddings, cluster.reshape(1, rows), slot.reshape(1, rows))


def centres_kernel(cen_hbm, centre_hbm, cen, centre_ref, in_sems, out_sems):
    parts = [pl.ds(i * CHUNK, CHUNK) for i in range(cen.shape[0] // CHUNK)]
    copies = [
        pltpu.make_async_copy(cen_hbm.at[part], cen.at[part], in_sems.at[i])
        for i, part in enumerate(parts)
    ]
    out = [
        pltpu.make_async_copy(centre_ref.at[part], centre_hbm.at[part], out_sems.at[i])
        for i, part in enumerate(parts)
    ]
    for copy in copies:
        copy.start()
    for i, part in enumerate(parts):
        copies[i].wait()
        centre_ref[part] = unit_of(cen[part])
        out[i].start()
    for copy in out:
        copy.wait()


def prepare_centres(centroids):
    count, width = centroids.shape
    return pl.pallas_call(
        centres_kernel,
        out_shape=jax.ShapeDtypeStruct((count, width), jnp.bfloat16),
        in_specs=[ANY],
        out_specs=ANY,
        scratch_shapes=[
            pltpu.VMEM((count, width), jnp.float32),
            pltpu.VMEM((count, width), jnp.bfloat16),
            pltpu.SemaphoreType.DMA((count // CHUNK,)),
            pltpu.SemaphoreType.DMA((count // CHUNK,)),
        ],
        compiler_params=PARAMS,
        cost_estimate=TINY,
        name="prepare_centres",
    )(centroids)


def score_kernel(rows_new, rows_kept, cents_new, cents_kept, priors, plan, keep, *refs):
    refs = list(refs)

    def take(n):
        head = refs[:n]
        del refs[:n]
        return head

    row_refs, cent_refs = take(len(rows_new)), take(len(cents_new))
    (kept_rows,) = take(1) if rows_kept else (None,)
    (kept_cents,) = take(1) if cents_kept else (None,)
    (prior_ref,) = take(1)
    (out_ref,) = take(1)
    rows, table, high, total, row_sems, cent_sems = refs

    def places(new, kept, buffer, kept_buffer):
        sources = [(buffer, sum(new[:i]), size) for i, size in enumerate(new)]
        return sources + [(kept_buffer, sum(kept[:i]), size) for i, size in enumerate(kept)]

    row_at = places(rows_new, rows_kept, rows, kept_rows)
    cent_at = places(cents_new, cents_kept, table, kept_cents)
    lane_at = [sum(size for _, _, size in row_at[:j]) for j in range(len(row_at))]

    def copies_of(arrays, sizes, buffer, sems):
        copies, i = [], 0
        for k, ref in enumerate(arrays):
            mine = []
            for start in range(0, sizes[k], STEP):
                place = pl.ds(sum(sizes[:k]) + start, STEP)
                mine.append(
                    pltpu.make_async_copy(ref.at[pl.ds(start, STEP)], buffer.at[place], sems.at[i])
                )
                i += 1
            copies.append(mine)
        return copies

    row_copies = copies_of(row_refs, rows_new, rows, row_sems)
    cent_copies = copies_of(cent_refs, cents_new, table, cent_sems)
    stages = [
        [copy for j in new_rows for copy in row_copies[j]]
        + [copy for i in new_cents for copy in cent_copies[i]]
        for new_rows, new_cents, _ in plan
    ]

    def product(i, j, cent, row):
        cents, cent_start, _ = cent_at[i]
        values, row_start, _ = row_at[j]
        return SCALE * lax.dot_general(
            cents[pl.ds(cent_start + cent, STEP)],
            values[pl.ds(row_start + row, LANES)],
            NT,
            preferred_element_type=jnp.float32,
        )

    def begin():
        base = 0
        for j, (_, _, size) in enumerate(row_at):
            lanes = slice(lane_at[j], lane_at[j] + size)
            if j in priors:
                first = lax.broadcasted_iota(jnp.int32, (8, size), 0) == 0
                high[:, lanes] = jnp.broadcast_to(prior_ref[:, base : base + size], (8, size))
                total[:, lanes] = jnp.where(first, 1.0, 0.0)
                base += size
            else:
                high[:, lanes] = jnp.full((8, size), -1e30, jnp.float32)
                total[:, lanes] = jnp.zeros((8, size), jnp.float32)

    for copy in stages[0]:
        copy.start()
    begin()
    begun = set(priors)
    for k, (_, _, products) in enumerate(plan):
        for copy in stages[k]:
            copy.wait()
        for copy in stages[k + 1] if k + 1 < len(plan) else []:
            copy.start()
        for i, j in products:
            for row in range(0, row_at[j][2], LANES):
                lanes = slice(lane_at[j] + row, lane_at[j] + row + LANES)
                for cent in range(0, cent_at[i][2], STEP):
                    value = product(i, j, cent, row)
                    if j not in begun and cent == 0:
                        shift = jnp.max(value, axis=0, keepdims=True)
                        high[:, lanes] = jnp.broadcast_to(shift, (8, LANES))
                    value = jnp.exp2(value.reshape(STEP // 8, 8, LANES) - high[:, lanes][None])
                    total[:, lanes] += jnp.sum(value, axis=0)
            begun.add(j)

    @pl.when(jnp.logical_not(jnp.max(total[...]) < 1e38))
    def _():
        begin()
        for i, j in [pair for _, _, products in plan for pair in products]:

            @pl.loop(0, row_at[j][2] // LANES)
            def _(r):
                @pl.loop(0, cent_at[i][2] // STEP)
                def _(c):
                    lanes = pl.ds(pl.multiple_of(lane_at[j] + r * LANES, LANES), LANES)
                    row, cent = pl.multiple_of(r * LANES, LANES), pl.multiple_of(c * STEP, STEP)
                    value = product(i, j, cent, row).reshape(STEP // 8, 8, LANES)
                    before = high[:, lanes]
                    now = jnp.maximum(before, jnp.max(value, axis=0))
                    high[:, lanes] = now
                    total[:, lanes] = total[:, lanes] * jnp.exp2(before - now) + jnp.sum(
                        jnp.exp2(value - now[None]), axis=0
                    )

    top = jnp.max(high[...], axis=0, keepdims=True)
    all_sum = jnp.sum(total[...] * jnp.exp2(high[...] - top), axis=0, keepdims=True)
    out_ref[...] = top + jnp.log2(all_sum)


def score(rows, centres, plan, name, vmem, prior=None, priors=(), kept=None, keep=False):
    width = (*rows, *centres)[0].shape[1]
    rows_new = tuple(value.shape[0] for value in rows)
    cents_new = tuple(value.shape[0] for value in centres)
    kept_rows, rows_kept, kept_cents, cents_kept = kept or (None, (), None, ())
    count = sum(rows_new) + sum(rows_kept)
    out = jax.ShapeDtypeStruct((1, count), jnp.float32)
    held = [(sum(rows_new) or 16, width), (sum(cents_new) or 16, width)]
    resident = [value for value in (kept_rows, kept_cents) if value is not None]
    if prior is None:
        prior = jnp.zeros((1, 128), jnp.float32)
    return pl.pallas_call(
        functools.partial(
            score_kernel, rows_new, rows_kept, cents_new, cents_kept, tuple(priors), plan, keep
        ),
        out_shape=(out, *[jax.ShapeDtypeStruct(shape, jnp.bfloat16) for shape in held])
        if keep
        else out,
        in_specs=[ANY] * (len(rows) + len(centres)) + [VMEM] * (len(resident) + 1),
        out_specs=(VMEM,) * 3 if keep else VMEM,
        scratch_shapes=([] if keep else [pltpu.VMEM(shape, jnp.bfloat16) for shape in held])
        + [
            pltpu.VMEM((8, count), jnp.float32),
            pltpu.VMEM((8, count), jnp.float32),
            pltpu.SemaphoreType.DMA((sum(rows_new) // STEP or 1,)),
            pltpu.SemaphoreType.DMA((sum(cents_new) // STEP,)),
        ],
        compiler_params=pltpu.CompilerParams(vmem_limit_bytes=vmem * 1024 * 1024),
        cost_estimate=pl.CostEstimate(flops=1 if name == "score_far" else 1, bytes_accessed=1, transcendentals=0),
        name=name,
    )(*(map(in_hbm, (*rows, *centres)) if kept is None else (*rows, *centres)), *resident, prior)


def owner_kernel(rows_hbm, out_ref, rows_ref, sems):
    total = rows_ref.shape[0]
    width = rows_ref.shape[1] - ID_LANES
    cap = out_ref.shape[1]
    block = LANES
    copies = [
        pltpu.make_async_copy(
            rows_hbm.at[pl.ds(i * block, block)], rows_ref.at[pl.ds(i * block, block)], sems.at[i]
        )
        for i in range(total // block)
    ]
    for copy in copies:
        copy.start()
    pick = (lax.broadcasted_iota(jnp.int32, (8, ID_LANES), 1) == 0).astype(jnp.float32)
    pick = pick.astype(jnp.bfloat16)
    r = lax.broadcasted_iota(jnp.int32, (block, block), 0)
    s = lax.broadcasted_iota(jnp.int32, (block, block), 1)
    eye = lax.broadcasted_iota(jnp.int32, (cap, ID_LANES), 0)
    eye = (eye == lax.broadcasted_iota(jnp.int32, (cap, ID_LANES), 1)).astype(jnp.float32)
    id_rows = []
    for row in range(0, total, block):
        if row in (0, total // 2):
            for copy in copies[row // block : (row + total // 2) // block]:
                copy.wait()
        ids = rows_ref[row : row + block, width:]
        id_rows.append(lax.dot_general(pick, ids, NT, preferred_element_type=jnp.float32)[:1])
        id_col = ids.astype(jnp.float32)
        best = jnp.full((block, ID_LANES), -1.0, jnp.float32)
        for col in range(0, row + block, block):
            gram = lax.dot_general(
                rows_ref[row : row + block, :width],
                rows_ref[col : col + block, :width],
                NT,
                preferred_element_type=jnp.float32,
            )
            for lane in range(0, block, ID_LANES):
                lanes = slice(lane, lane + ID_LANES)
                same = id_col == id_rows[col // block][:, lanes]
                if row == col:
                    same = same & (s < r)[:, lanes]
                best = jnp.maximum(best, jnp.where(same, gram[:, lanes], -1.0))
        best = jnp.max(best, axis=1, keepdims=True).reshape(block // cap, cap, 1)
        best = jnp.sum(best * eye[None], axis=1)
        out_ref[row // cap : (row + block) // cap, :] = best[:, :cap]


def owner_best(rows, cap):
    total, width = rows.shape
    return pl.pallas_call(
        owner_kernel,
        out_shape=jax.ShapeDtypeStruct((total // cap, cap), jnp.float32),
        in_specs=[ANY],
        out_specs=VMEM,
        scratch_shapes=[
            pltpu.VMEM((total, width), jnp.bfloat16),
            pltpu.SemaphoreType.DMA((total // LANES,)),
        ],
        compiler_params=SCORE_PARAMS,
        cost_estimate=TINY,
        name="owner_best",
    )(rows)


def pick_kernel(per_owner, got_ref, cluster_ref, slot_ref, out_ref):
    got = got_ref[...]
    devices, cap = got.shape
    rows = out_ref.shape[1]
    owner = cluster_ref[...] // per_owner
    hot = (lax.broadcasted_iota(jnp.int32, (devices, rows), 0) == owner).astype(jnp.float32)
    by_slot = lax.dot_general(
        got,
        hot,
        (((0,), (0,)), ((), ())),
        precision=lax.Precision.HIGHEST,
        preferred_element_type=jnp.float32,
    )
    mine = lax.broadcasted_iota(jnp.int32, (cap, rows), 0) == slot_ref[...]
    out_ref[...] = jnp.sum(jnp.where(mine, by_slot, 0.0), axis=0, keepdims=True)


def pick(got, cluster, slot, per_owner):
    rows = cluster.shape[0]
    return pl.pallas_call(
        functools.partial(pick_kernel, per_owner),
        out_shape=jax.ShapeDtypeStruct((1, rows), jnp.float32),
        in_specs=[VMEM] * 3,
        out_specs=VMEM,
        compiler_params=SCORE_PARAMS,
        cost_estimate=TINY,
        name="pick",
    )(got, cluster.reshape(1, rows), slot.reshape(1, rows)).reshape(rows)


def move(value, step):
    pairs = []
    for y in range(4):
        for x in range(4):
            for z in range(4):
                for core in range(2):
                    here, there = [
                        (y * 2 + a % 4 // 2) * 16 + (b % 4 * 2 + a % 2) * 2 + c
                        for a, b, c in ((x, z, core), step(x, z, core))
                    ]
                    pairs.append((here, there))
    return lax.ppermute(value, ("doc", "cent"), pairs)


def swap_core(value):
    return move(value, lambda x, z, core: (x, z, 1 - core))


def move_x(value):
    return move(value, lambda x, z, core: (x + 1 - 2 * core, z, core))


def move_z(value, by):
    return move(value, lambda x, z, core: (x, z + by * (1 - 2 * core), core))


def per_device(embeddings, centroids, cluster, slot):
    row_count, width = embeddings.shape
    devices = lax.axis_size("doc") * lax.axis_size("cent")
    per_owner = centroids.shape[0] // lax.axis_size("doc")
    cap = 2 * row_count // devices

    unit, send = prepare_rows(embeddings, cluster, slot, per_owner, cap, devices)
    centre = prepare_centres(lax.optimization_barrier((centroids, unit))[0])
    ahead, behind = move_z(unit, 1), move_z(unit, -1)
    side, core = move_x(centre), swap_core(centre)
    plan = (((0,), (0,), ((0, 0),)), ((), (1,), ((1, 0),)))
    first = score((unit,), (centre, core), plan, "score_own", 24)

    def after(value, done):
        return lax.optimization_barrier((value, done))[0]

    got = lax.all_to_all(
        send.reshape(devices, cap, width + ID_LANES),
        ("doc", "cent"),
        split_axis=0,
        concat_axis=0,
        tiled=True,
    )
    best = owner_best(after(got, first).reshape(devices * cap, width + ID_LANES), cap)
    returned = lax.all_to_all(best, ("doc", "cent"), split_axis=0, concat_axis=0, tiled=True)

    side, ahead, behind = after(side, returned), after(ahead, returned), after(behind, returned)
    side_core = swap_core(after(side, (ahead, behind)))
    far = move_z(ahead, 1)
    plan = (
        ((0, 1), (0,), ((0, 0), (0, 1))),
        ((2,), (1,), ((0, 2), (1, 1), (1, 2))),
        ((), (2,), ((2, 1), (2, 2))),
    )
    near, rows, table = score(
        (unit, ahead, behind),
        (side, centre, core),
        plan,
        "score_near",
        24,
        prior=first,
        priors=(0,),
        keep=True,
    )
    plan = (((), (0,), ((0, 0), (0, 1), (0, 2))),)
    sizes = (row_count,) * 3
    mid = score(
        (), (side_core,), plan, "score_mid", 16, prior=near, priors=(0, 1, 2), kept=(rows, sizes, None, ())
    )
    parts = [mid[:, i * row_count : (i + 1) * row_count] for i in range(3)]
    dup_sim = pick(after(returned, near), cluster, slot, per_owner)
    plan = (((0,), (), ((1, 0), (2, 0), (3, 0))), ((), (0,), ((0, 0),)))
    kept = (None, (), table, (centre.shape[0],) * 3)
    last = score((after(far, (mid, dup_sim)),), (side_core,), plan, "score_far", 16, kept=kept)
    terms = (move_z(last, 2), parts[0], move_z(parts[1], -1), move_z(parts[2], 1))
    terms = jnp.concatenate(terms, axis=0)
    top = jnp.max(terms, axis=0)
    soft_cost = 1.0 - BACK * (top + jnp.log2(jnp.sum(jnp.exp2(terms - top[None]), axis=0)))
    return (soft_cost, dup_sim)


def solution(mesh):
    return jax.shard_map(
        per_device,
        mesh=mesh,
        in_specs=(
            P(("doc", "cent"), None),
            P("cent", None),
            P(("doc", "cent")),
            P(("doc", "cent")),
        ),
        out_specs=(P(("doc", "cent")), P(("doc", "cent"))),
        check_vma=False,
    )
```

```python
import functools
import math

import jax
import jax.numpy as jnp
from jax import lax
from jax.experimental import pallas as pl
from jax.experimental.pallas import tpu as pltpu
from jax.sharding import PartitionSpec as P

INVERSE_TEMP = 256.0
SCALE = INVERSE_TEMP / math.log(2.0)
BACK = math.log(2.0) / INVERSE_TEMP
NT = (((1,), (1,)), ((), ()))
ID_LANES = 128
LANES = 256
VMEM = pl.BlockSpec(memory_space=pltpu.VMEM)
TINY = pl.CostEstimate(flops=1, bytes_accessed=1, transcendentals=0)


PARAMS = pltpu.CompilerParams(vmem_limit_bytes=60 * 1024 * 1024)
SCORE_PARAMS = pltpu.CompilerParams(vmem_limit_bytes=24 * 1024 * 1024)
ANY = pl.BlockSpec(memory_space=pl.ANY)
CHUNK = 128
STEP = 512
TILE = 1024


def in_hbm(value):
    return pltpu.with_memory_space_constraint(value, pltpu.HBM)


def unit_of(values):
    total = jnp.sum(values * values, axis=1, keepdims=True)
    return (values * lax.rsqrt(total + 1e-06)).astype(jnp.bfloat16)


def rows_kernel(per_owner, cap, *refs):
    emb_hbm, cluster_hbm, slot_hbm, unit_hbm, send_hbm = refs[:5]
    emb, cluster_ref, slot_ref, unit_ref, send_ref = refs[5:10]
    emb_sems, id_sems, unit_sems, send_sems = refs[10:]
    rows, width = emb.shape

    def piece(ref, i, size=CHUNK):
        return ref.at[pl.ds(i * size, size)]

    ids = [
        pltpu.make_async_copy(cluster_hbm, cluster_ref, id_sems.at[0]),
        pltpu.make_async_copy(slot_hbm, slot_ref, id_sems.at[1]),
    ]
    emb_copies = [
        pltpu.make_async_copy(piece(emb_hbm, i), piece(emb, i), emb_sems.at[i])
        for i in range(rows // CHUNK)
    ]
    for copy in emb_copies + ids:
        copy.start()
    out = []

    def send_out(src, dst, sem):
        out.append(pltpu.make_async_copy(src, dst, sem))
        out[-1].start()

    for i, copy in enumerate(emb_copies):
        copy.wait()
        part = slice(i * CHUNK, (i + 1) * CHUNK)
        unit_ref[part] = unit_of(emb[part])
        send_out(piece(unit_ref, i), piece(unit_hbm, i), unit_sems.at[i])
    for copy in ids:
        copy.wait()
    cluster = cluster_ref[...]
    target = (cluster // per_owner) * cap + slot_ref[...]
    local = (cluster % per_owner + 1).astype(jnp.float32)
    names = jnp.broadcast_to(local, (ID_LANES, rows)).astype(jnp.bfloat16)
    for i in range(send_ref.shape[0] // LANES):
        part = slice(i * LANES, (i + 1) * LANES)
        place = i * LANES + lax.broadcasted_iota(jnp.int32, (LANES, rows), 0)
        hot = (place == target).astype(jnp.float32).astype(jnp.bfloat16)
        send_ref[part, :width] = lax.dot_general(
            hot, unit_ref[...], (((1,), (0,)), ((), ())), preferred_element_type=jnp.float32
        ).astype(jnp.bfloat16)
        send_ref[part, width:] = (
            lax.dot_general(hot, names, NT, preferred_element_type=jnp.float32) - 1.0
        ).astype(jnp.bfloat16)
        send_out(piece(send_ref, i, LANES), piece(send_hbm, i, LANES), send_sems.at[i])
    for copy in out:
        copy.wait()


def prepare_rows(embeddings, cluster, slot, per_owner, cap, devices):
    rows, width = embeddings.shape
    send = (devices * cap, width + ID_LANES)
    return pl.pallas_call(
        functools.partial(rows_kernel, per_owner, cap),
        out_shape=tuple(jax.ShapeDtypeStruct(shape, jnp.bfloat16) for shape in ((rows, width), send)),
        in_specs=[ANY] * 3,
        out_specs=(ANY,) * 2,
        scratch_shapes=[
            pltpu.VMEM((rows, width), jnp.float32),
            pltpu.VMEM((1, rows), jnp.int32),
            pltpu.VMEM((1, rows), jnp.int32),
            pltpu.VMEM((rows, width), jnp.bfloat16),
            pltpu.VMEM(send, jnp.bfloat16),
        ]
        + [pltpu.SemaphoreType.DMA((n,)) for n in (rows // CHUNK, 2, rows // CHUNK, send[0] // LANES)],
        compiler_params=PARAMS,
        cost_estimate=TINY,
        name="prepare_rows",
    )(embeddings, cluster.reshape(1, rows), slot.reshape(1, rows))


def centres_kernel(cen_hbm, centre_hbm, cen, centre_ref, in_sems, out_sems):
    parts = [pl.ds(i * CHUNK, CHUNK) for i in range(cen.shape[0] // CHUNK)]
    copies = [
        pltpu.make_async_copy(cen_hbm.at[part], cen.at[part], in_sems.at[i])
        for i, part in enumerate(parts)
    ]
    out = [
        pltpu.make_async_copy(centre_ref.at[part], centre_hbm.at[part], out_sems.at[i])
        for i, part in enumerate(parts)
    ]
    for copy in copies:
        copy.start()
    for i, part in enumerate(parts):
        copies[i].wait()
        centre_ref[part] = unit_of(cen[part])
        out[i].start()
    for copy in out:
        copy.wait()


def prepare_centres(centroids):
    count, width = centroids.shape
    return pl.pallas_call(
        centres_kernel,
        out_shape=jax.ShapeDtypeStruct((count, width), jnp.bfloat16),
        in_specs=[ANY],
        out_specs=ANY,
        scratch_shapes=[
            pltpu.VMEM((count, width), jnp.float32),
            pltpu.VMEM((count, width), jnp.bfloat16),
            pltpu.SemaphoreType.DMA((count // CHUNK,)),
            pltpu.SemaphoreType.DMA((count // CHUNK,)),
        ],
        compiler_params=PARAMS,
        cost_estimate=TINY,
        name="prepare_centres",
    )(centroids)


def score_kernel(rows_new, rows_kept, cents_new, cents_kept, priors, plan, keep, *refs):
    refs = list(refs)

    def take(n):
        head = refs[:n]
        del refs[:n]
        return head

    row_refs, cent_refs = take(len(rows_new)), take(len(cents_new))
    (kept_rows,) = take(1) if rows_kept else (None,)
    (kept_cents,) = take(1) if cents_kept else (None,)
    (prior_ref,) = take(1)
    (out_ref,) = take(1)
    rows, table, high, total, row_sems, cent_sems = refs

    def places(new, kept, buffer, kept_buffer):
        sources = [(buffer, sum(new[:i]), size) for i, size in enumerate(new)]
        return sources + [(kept_buffer, sum(kept[:i]), size) for i, size in enumerate(kept)]

    row_at = places(rows_new, rows_kept, rows, kept_rows)
    cent_at = places(cents_new, cents_kept, table, kept_cents)
    lane_at = [sum(size for _, _, size in row_at[:j]) for j in range(len(row_at))]

    def copies_of(arrays, sizes, buffer, sems):
        copies, i = [], 0
        for k, ref in enumerate(arrays):
            mine = []
            for start in range(0, sizes[k], STEP):
                place = pl.ds(sum(sizes[:k]) + start, STEP)
                mine.append(
                    pltpu.make_async_copy(ref.at[pl.ds(start, STEP)], buffer.at[place], sems.at[i])
                )
                i += 1
            copies.append(mine)
        return copies

    row_copies = copies_of(row_refs, rows_new, rows, row_sems)
    cent_copies = copies_of(cent_refs, cents_new, table, cent_sems)
    stages = [
        [copy for j in new_rows for copy in row_copies[j]]
        + [copy for i in new_cents for copy in cent_copies[i]]
        for new_rows, new_cents, _ in plan
    ]

    def product(i, j, cent, row):
        cents, cent_start, _ = cent_at[i]
        values, row_start, _ = row_at[j]
        return SCALE * lax.dot_general(
            cents[pl.ds(cent_start + cent, TILE)],
            values[pl.ds(row_start + row, LANES)],
            NT,
            preferred_element_type=jnp.float32,
        )

    def begin():
        base = 0
        for j, (_, _, size) in enumerate(row_at):
            lanes = slice(lane_at[j], lane_at[j] + size)
            if j in priors:
                first = lax.broadcasted_iota(jnp.int32, (8, size), 0) == 0
                high[:, lanes] = jnp.broadcast_to(prior_ref[:, base : base + size], (8, size))
                total[:, lanes] = jnp.where(first, 1.0, 0.0)
                base += size
            else:
                high[:, lanes] = jnp.full((8, size), -1e30, jnp.float32)
                total[:, lanes] = jnp.zeros((8, size), jnp.float32)

    for copy in stages[0]:
        copy.start()
    begin()
    begun = set(priors)
    for k, (_, _, products) in enumerate(plan):
        for copy in stages[k]:
            copy.wait()
        for copy in stages[k + 1] if k + 1 < len(plan) else []:
            copy.start()
        for i, j in products:
            for row in range(0, row_at[j][2], LANES):
                lanes = slice(lane_at[j] + row, lane_at[j] + row + LANES)
                for cent in range(0, cent_at[i][2], TILE):
                    value = product(i, j, cent, row)
                    if j not in begun and cent == 0:
                        shift = jnp.max(value, axis=0, keepdims=True)
                        high[:, lanes] = jnp.broadcast_to(shift, (8, LANES))
                    value = jnp.exp2(value.reshape(TILE // 8, 8, LANES) - high[:, lanes][None])
                    total[:, lanes] += jnp.sum(value, axis=0)
            begun.add(j)

    @pl.when(jnp.logical_not(jnp.max(total[...]) < 1e38))
    def _():
        begin()
        for i, j in [pair for _, _, products in plan for pair in products]:

            @pl.loop(0, row_at[j][2] // LANES)
            def _(r):
                @pl.loop(0, cent_at[i][2] // TILE)
                def _(c):
                    lanes = pl.ds(pl.multiple_of(lane_at[j] + r * LANES, LANES), LANES)
                    row, cent = pl.multiple_of(r * LANES, LANES), pl.multiple_of(c * TILE, TILE)
                    value = product(i, j, cent, row).reshape(TILE // 8, 8, LANES)
                    before = high[:, lanes]
                    now = jnp.maximum(before, jnp.max(value, axis=0))
                    high[:, lanes] = now
                    total[:, lanes] = total[:, lanes] * jnp.exp2(before - now) + jnp.sum(
                        jnp.exp2(value - now[None]), axis=0
                    )

    top = jnp.max(high[...], axis=0, keepdims=True)
    all_sum = jnp.sum(total[...] * jnp.exp2(high[...] - top), axis=0, keepdims=True)
    out_ref[...] = top + jnp.log2(all_sum)


def score(rows, centres, plan, name, vmem, prior=None, priors=(), kept=None, keep=False):
    width = (*rows, *centres)[0].shape[1]
    rows_new = tuple(value.shape[0] for value in rows)
    cents_new = tuple(value.shape[0] for value in centres)
    kept_rows, rows_kept, kept_cents, cents_kept = kept or (None, (), None, ())
    count = sum(rows_new) + sum(rows_kept)
    out = jax.ShapeDtypeStruct((1, count), jnp.float32)
    held = [(sum(rows_new) or 16, width), (sum(cents_new) or 16, width)]
    resident = [value for value in (kept_rows, kept_cents) if value is not None]
    if prior is None:
        prior = jnp.zeros((1, 128), jnp.float32)
    return pl.pallas_call(
        functools.partial(
            score_kernel, rows_new, rows_kept, cents_new, cents_kept, tuple(priors), plan, keep
        ),
        out_shape=(out, *[jax.ShapeDtypeStruct(shape, jnp.bfloat16) for shape in held])
        if keep
        else out,
        in_specs=[ANY] * (len(rows) + len(centres)) + [VMEM] * (len(resident) + 1),
        out_specs=(VMEM,) * 3 if keep else VMEM,
        scratch_shapes=([] if keep else [pltpu.VMEM(shape, jnp.bfloat16) for shape in held])
        + [
            pltpu.VMEM((8, count), jnp.float32),
            pltpu.VMEM((8, count), jnp.float32),
            pltpu.SemaphoreType.DMA((sum(rows_new) // STEP or 1,)),
            pltpu.SemaphoreType.DMA((sum(cents_new) // STEP,)),
        ],
        compiler_params=pltpu.CompilerParams(vmem_limit_bytes=vmem * 1024 * 1024),
        cost_estimate=pl.CostEstimate(flops=1 if name == "score_far" else 1, bytes_accessed=1, transcendentals=0),
        name=name,
    )(*(map(in_hbm, (*rows, *centres)) if kept is None else (*rows, *centres)), *resident, prior)


def owner_kernel(rows_hbm, out_ref, rows_ref, sems):
    total = rows_ref.shape[0]
    width = rows_ref.shape[1] - ID_LANES
    cap = out_ref.shape[1]
    block = LANES
    copies = [
        pltpu.make_async_copy(
            rows_hbm.at[pl.ds(i * block, block)], rows_ref.at[pl.ds(i * block, block)], sems.at[i]
        )
        for i in range(total // block)
    ]
    for copy in copies:
        copy.start()
    pick = (lax.broadcasted_iota(jnp.int32, (8, ID_LANES), 1) == 0).astype(jnp.float32)
    pick = pick.astype(jnp.bfloat16)
    r = lax.broadcasted_iota(jnp.int32, (block, block), 0)
    s = lax.broadcasted_iota(jnp.int32, (block, block), 1)
    eye = lax.broadcasted_iota(jnp.int32, (cap, ID_LANES), 0)
    eye = (eye == lax.broadcasted_iota(jnp.int32, (cap, ID_LANES), 1)).astype(jnp.float32)
    id_rows = []
    for row in range(0, total, block):
        if row in (0, total // 2):
            for copy in copies[row // block : (row + total // 2) // block]:
                copy.wait()
        ids = rows_ref[row : row + block, width:]
        id_rows.append(lax.dot_general(pick, ids, NT, preferred_element_type=jnp.float32)[:1])
        id_col = ids.astype(jnp.float32)
        best = jnp.full((block, ID_LANES), -1.0, jnp.float32)
        for col in range(0, row + block, block):
            gram = lax.dot_general(
                rows_ref[row : row + block, :width],
                rows_ref[col : col + block, :width],
                NT,
                preferred_element_type=jnp.float32,
            )
            for lane in range(0, block, ID_LANES):
                lanes = slice(lane, lane + ID_LANES)
                same = id_col == id_rows[col // block][:, lanes]
                if row == col:
                    same = same & (s < r)[:, lanes]
                best = jnp.maximum(best, jnp.where(same, gram[:, lanes], -1.0))
        best = jnp.max(best, axis=1, keepdims=True).reshape(block // cap, cap, 1)
        best = jnp.sum(best * eye[None], axis=1)
        out_ref[row // cap : (row + block) // cap, :] = best[:, :cap]


def owner_best(rows, cap):
    total, width = rows.shape
    return pl.pallas_call(
        owner_kernel,
        out_shape=jax.ShapeDtypeStruct((total // cap, cap), jnp.float32),
        in_specs=[ANY],
        out_specs=VMEM,
        scratch_shapes=[
            pltpu.VMEM((total, width), jnp.bfloat16),
            pltpu.SemaphoreType.DMA((total // LANES,)),
        ],
        compiler_params=SCORE_PARAMS,
        cost_estimate=TINY,
        name="owner_best",
    )(rows)


def pick_kernel(per_owner, got_ref, cluster_ref, slot_ref, out_ref):
    got = got_ref[...]
    devices, cap = got.shape
    rows = out_ref.shape[1]
    owner = cluster_ref[...] // per_owner
    hot = (lax.broadcasted_iota(jnp.int32, (devices, rows), 0) == owner).astype(jnp.float32)
    by_slot = lax.dot_general(
        got,
        hot,
        (((0,), (0,)), ((), ())),
        precision=lax.Precision.HIGHEST,
        preferred_element_type=jnp.float32,
    )
    mine = lax.broadcasted_iota(jnp.int32, (cap, rows), 0) == slot_ref[...]
    out_ref[...] = jnp.sum(jnp.where(mine, by_slot, 0.0), axis=0, keepdims=True)


def pick(got, cluster, slot, per_owner):
    rows = cluster.shape[0]
    return pl.pallas_call(
        functools.partial(pick_kernel, per_owner),
        out_shape=jax.ShapeDtypeStruct((1, rows), jnp.float32),
        in_specs=[VMEM] * 3,
        out_specs=VMEM,
        compiler_params=SCORE_PARAMS,
        cost_estimate=TINY,
        name="pick",
    )(got, cluster.reshape(1, rows), slot.reshape(1, rows)).reshape(rows)


def move(value, step):
    pairs = []
    for y in range(4):
        for x in range(4):
            for z in range(4):
                for core in range(2):
                    here, there = [
                        (y * 2 + a % 4 // 2) * 16 + (b % 4 * 2 + a % 2) * 2 + c
                        for a, b, c in ((x, z, core), step(x, z, core))
                    ]
                    pairs.append((here, there))
    return lax.ppermute(value, ("doc", "cent"), pairs)


def swap_core(value):
    return move(value, lambda x, z, core: (x, z, 1 - core))


def move_x(value):
    return move(value, lambda x, z, core: (x + 1 - 2 * core, z, core))


def move_z(value, by):
    return move(value, lambda x, z, core: (x, z + by * (1 - 2 * core), core))


def per_device(embeddings, centroids, cluster, slot):
    row_count, width = embeddings.shape
    devices = lax.axis_size("doc") * lax.axis_size("cent")
    per_owner = centroids.shape[0] // lax.axis_size("doc")
    cap = 2 * row_count // devices

    unit, send = prepare_rows(embeddings, cluster, slot, per_owner, cap, devices)
    centre = prepare_centres(lax.optimization_barrier((centroids, unit))[0])
    ahead, behind = move_z(unit, 1), move_z(unit, -1)
    side, core = move_x(centre), swap_core(centre)
    plan = (((0,), (0,), ((0, 0),)), ((), (1,), ((1, 0),)))
    first = score((unit,), (centre, core), plan, "score_own", 24)

    def after(value, done):
        return lax.optimization_barrier((value, done))[0]

    got = lax.all_to_all(
        send.reshape(devices, cap, width + ID_LANES),
        ("doc", "cent"),
        split_axis=0,
        concat_axis=0,
        tiled=True,
    )
    best = owner_best(after(got, first).reshape(devices * cap, width + ID_LANES), cap)
    returned = lax.all_to_all(best, ("doc", "cent"), split_axis=0, concat_axis=0, tiled=True)

    side, ahead, behind = after(side, returned), after(ahead, returned), after(behind, returned)
    side_core = swap_core(after(side, (ahead, behind)))
    far = move_z(ahead, 1)
    plan = (
        ((0, 1), (0,), ((0, 0), (0, 1))),
        ((2,), (1,), ((0, 2), (1, 1), (1, 2))),
        ((), (2,), ((2, 1), (2, 2))),
    )
    near, rows, table = score(
        (unit, ahead, behind),
        (side, centre, core),
        plan,
        "score_near",
        24,
        prior=first,
        priors=(0,),
        keep=True,
    )
    plan = (((), (0,), ((0, 0), (0, 1), (0, 2))),)
    sizes = (row_count,) * 3
    mid = score(
        (), (side_core,), plan, "score_mid", 16, prior=near, priors=(0, 1, 2), kept=(rows, sizes, None, ())
    )
    parts = [mid[:, i * row_count : (i + 1) * row_count] for i in range(3)]
    plan = (((0,), (), ((1, 0), (2, 0), (3, 0))), ((), (0,), ((0, 0),)))
    kept = (None, (), table, (centre.shape[0],) * 3)
    last = score((after(far, mid),), (side_core,), plan, "score_far", 16, kept=kept)
    dup_sim = pick(after(returned, last), cluster, slot, per_owner)
    terms = (move_z(last, 2), parts[0], move_z(parts[1], -1), move_z(parts[2], 1))
    terms = jnp.concatenate(terms, axis=0)
    top = jnp.max(terms, axis=0)
    soft_cost = 1.0 - BACK * (top + jnp.log2(jnp.sum(jnp.exp2(terms - top[None]), axis=0)))
    return (soft_cost, dup_sim)


def solution(mesh):
    return jax.shard_map(
        per_device,
        mesh=mesh,
        in_specs=(
            P(("doc", "cent"), None),
            P("cent", None),
            P(("doc", "cent")),
            P(("doc", "cent")),
        ),
        out_specs=(P(("doc", "cent")), P(("doc", "cent"))),
        check_vma=False,
    )
```

```python
import functools
import math

import jax
import jax.numpy as jnp
from jax import lax
from jax.experimental import pallas as pl
from jax.experimental.pallas import tpu as pltpu
from jax.sharding import PartitionSpec as P

INVERSE_TEMP = 256.0
SCALE = INVERSE_TEMP / math.log(2.0)
BACK = math.log(2.0) / INVERSE_TEMP
NT = (((1,), (1,)), ((), ()))
ID_LANES = 128
LANES = 256
VMEM = pl.BlockSpec(memory_space=pltpu.VMEM)
TINY = pl.CostEstimate(flops=1, bytes_accessed=1, transcendentals=0)


PARAMS = pltpu.CompilerParams(vmem_limit_bytes=60 * 1024 * 1024)
SCORE_PARAMS = pltpu.CompilerParams(vmem_limit_bytes=24 * 1024 * 1024)
ANY = pl.BlockSpec(memory_space=pl.ANY)
CHUNK = 256
STEP = 512
TILE = 1024


def in_hbm(value):
    return pltpu.with_memory_space_constraint(value, pltpu.HBM)


def unit_of(values):
    total = jnp.sum(values * values, axis=1, keepdims=True)
    return (values * lax.rsqrt(total + 1e-06)).astype(jnp.bfloat16)


def rows_kernel(per_owner, cap, *refs):
    emb_hbm, cluster_hbm, slot_hbm, unit_hbm, send_hbm = refs[:5]
    emb, cluster_ref, slot_ref, unit_ref, send_ref = refs[5:10]
    emb_sems, id_sems, unit_sems, send_sems = refs[10:]
    rows, width = emb.shape

    def piece(ref, i, size=CHUNK):
        return ref.at[pl.ds(i * size, size)]

    ids = [
        pltpu.make_async_copy(cluster_hbm, cluster_ref, id_sems.at[0]),
        pltpu.make_async_copy(slot_hbm, slot_ref, id_sems.at[1]),
    ]
    emb_copies = [
        pltpu.make_async_copy(piece(emb_hbm, i), piece(emb, i), emb_sems.at[i])
        for i in range(rows // CHUNK)
    ]
    for copy in emb_copies + ids:
        copy.start()
    out = []

    def send_out(src, dst, sem):
        out.append(pltpu.make_async_copy(src, dst, sem))
        out[-1].start()

    for i, copy in enumerate(emb_copies):
        copy.wait()
        part = slice(i * CHUNK, (i + 1) * CHUNK)
        unit_ref[part] = unit_of(emb[part])
        send_out(piece(unit_ref, i), piece(unit_hbm, i), unit_sems.at[i])
    for copy in ids:
        copy.wait()
    cluster = cluster_ref[...]
    target = (cluster // per_owner) * cap + slot_ref[...]
    local = (cluster % per_owner + 1).astype(jnp.float32)
    names = jnp.broadcast_to(local, (ID_LANES, rows)).astype(jnp.bfloat16)
    for i in range(send_ref.shape[0] // LANES):
        part = slice(i * LANES, (i + 1) * LANES)
        place = i * LANES + lax.broadcasted_iota(jnp.int32, (LANES, rows), 0)
        hot = (place == target).astype(jnp.float32).astype(jnp.bfloat16)
        send_ref[part, :width] = lax.dot_general(
            hot, unit_ref[...], (((1,), (0,)), ((), ())), preferred_element_type=jnp.float32
        ).astype(jnp.bfloat16)
        send_ref[part, width:] = (
            lax.dot_general(hot, names, NT, preferred_element_type=jnp.float32) - 1.0
        ).astype(jnp.bfloat16)
        send_out(piece(send_ref, i, LANES), piece(send_hbm, i, LANES), send_sems.at[i])
    for copy in out:
        copy.wait()


def prepare_rows(embeddings, cluster, slot, per_owner, cap, devices):
    rows, width = embeddings.shape
    send = (devices * cap, width + ID_LANES)
    return pl.pallas_call(
        functools.partial(rows_kernel, per_owner, cap),
        out_shape=tuple(jax.ShapeDtypeStruct(shape, jnp.bfloat16) for shape in ((rows, width), send)),
        in_specs=[ANY] * 3,
        out_specs=(ANY,) * 2,
        scratch_shapes=[
            pltpu.VMEM((rows, width), jnp.float32),
            pltpu.VMEM((1, rows), jnp.int32),
            pltpu.VMEM((1, rows), jnp.int32),
            pltpu.VMEM((rows, width), jnp.bfloat16),
            pltpu.VMEM(send, jnp.bfloat16),
        ]
        + [pltpu.SemaphoreType.DMA((n,)) for n in (rows // CHUNK, 2, rows // CHUNK, send[0] // LANES)],
        compiler_params=PARAMS,
        cost_estimate=TINY,
        name="prepare_rows",
    )(embeddings, cluster.reshape(1, rows), slot.reshape(1, rows))


def centres_kernel(cen_hbm, centre_hbm, cen, centre_ref, in_sems, out_sems):
    parts = [pl.ds(i * CHUNK, CHUNK) for i in range(cen.shape[0] // CHUNK)]
    copies = [
        pltpu.make_async_copy(cen_hbm.at[part], cen.at[part], in_sems.at[i])
        for i, part in enumerate(parts)
    ]
    out = [
        pltpu.make_async_copy(centre_ref.at[part], centre_hbm.at[part], out_sems.at[i])
        for i, part in enumerate(parts)
    ]
    for copy in copies:
        copy.start()
    for i, part in enumerate(parts):
        copies[i].wait()
        centre_ref[part] = unit_of(cen[part])
        out[i].start()
    for copy in out:
        copy.wait()


def prepare_centres(centroids):
    count, width = centroids.shape
    return pl.pallas_call(
        centres_kernel,
        out_shape=jax.ShapeDtypeStruct((count, width), jnp.bfloat16),
        in_specs=[ANY],
        out_specs=ANY,
        scratch_shapes=[
            pltpu.VMEM((count, width), jnp.float32),
            pltpu.VMEM((count, width), jnp.bfloat16),
            pltpu.SemaphoreType.DMA((count // CHUNK,)),
            pltpu.SemaphoreType.DMA((count // CHUNK,)),
        ],
        compiler_params=PARAMS,
        cost_estimate=TINY,
        name="prepare_centres",
    )(centroids)


def score_kernel(rows_new, rows_kept, cents_new, cents_kept, priors, plan, keep, *refs):
    refs = list(refs)

    def take(n):
        head = refs[:n]
        del refs[:n]
        return head

    row_refs, cent_refs = take(len(rows_new)), take(len(cents_new))
    (kept_rows,) = take(1) if rows_kept else (None,)
    (kept_cents,) = take(1) if cents_kept else (None,)
    (prior_ref,) = take(1)
    (out_ref,) = take(1)
    rows, table, high, total, row_sems, cent_sems = refs

    def places(new, kept, buffer, kept_buffer):
        sources = [(buffer, sum(new[:i]), size) for i, size in enumerate(new)]
        return sources + [(kept_buffer, sum(kept[:i]), size) for i, size in enumerate(kept)]

    row_at = places(rows_new, rows_kept, rows, kept_rows)
    cent_at = places(cents_new, cents_kept, table, kept_cents)
    lane_at = [sum(size for _, _, size in row_at[:j]) for j in range(len(row_at))]

    def copies_of(arrays, sizes, buffer, sems):
        copies, i = [], 0
        for k, ref in enumerate(arrays):
            mine = []
            for start in range(0, sizes[k], STEP):
                place = pl.ds(sum(sizes[:k]) + start, STEP)
                mine.append(
                    pltpu.make_async_copy(ref.at[pl.ds(start, STEP)], buffer.at[place], sems.at[i])
                )
                i += 1
            copies.append(mine)
        return copies

    row_copies = copies_of(row_refs, rows_new, rows, row_sems)
    cent_copies = copies_of(cent_refs, cents_new, table, cent_sems)
    stages = [
        [copy for j in new_rows for copy in row_copies[j]]
        + [copy for i in new_cents for copy in cent_copies[i]]
        for new_rows, new_cents, _ in plan
    ]

    def product(i, j, cent, row):
        cents, cent_start, _ = cent_at[i]
        values, row_start, _ = row_at[j]
        return SCALE * lax.dot_general(
            cents[pl.ds(cent_start + cent, TILE)],
            values[pl.ds(row_start + row, LANES)],
            NT,
            preferred_element_type=jnp.float32,
        )

    def begin():
        base = 0
        for j, (_, _, size) in enumerate(row_at):
            lanes = slice(lane_at[j], lane_at[j] + size)
            if j in priors:
                first = lax.broadcasted_iota(jnp.int32, (8, size), 0) == 0
                high[:, lanes] = jnp.broadcast_to(prior_ref[:, base : base + size], (8, size))
                total[:, lanes] = jnp.where(first, 1.0, 0.0)
                base += size
            else:
                high[:, lanes] = jnp.full((8, size), -1e30, jnp.float32)
                total[:, lanes] = jnp.zeros((8, size), jnp.float32)

    for copy in stages[0]:
        copy.start()
    begin()
    begun = set(priors)
    for k, (_, _, products) in enumerate(plan):
        for copy in stages[k]:
            copy.wait()
        for copy in stages[k + 1] if k + 1 < len(plan) else []:
            copy.start()
        for i, j in products:
            for row in range(0, row_at[j][2], LANES):
                lanes = slice(lane_at[j] + row, lane_at[j] + row + LANES)
                for cent in range(0, cent_at[i][2], TILE):
                    value = product(i, j, cent, row)
                    if j not in begun and cent == 0:
                        shift = jnp.max(value, axis=0, keepdims=True)
                        high[:, lanes] = jnp.broadcast_to(shift, (8, LANES))
                    value = jnp.exp2(value.reshape(TILE // 8, 8, LANES) - high[:, lanes][None])
                    total[:, lanes] += jnp.sum(value, axis=0)
            begun.add(j)

    @pl.when(jnp.logical_not(jnp.max(total[...]) < 1e38))
    def _():
        begin()
        for i, j in [pair for _, _, products in plan for pair in products]:

            @pl.loop(0, row_at[j][2] // LANES)
            def _(r):
                @pl.loop(0, cent_at[i][2] // TILE)
                def _(c):
                    lanes = pl.ds(pl.multiple_of(lane_at[j] + r * LANES, LANES), LANES)
                    row, cent = pl.multiple_of(r * LANES, LANES), pl.multiple_of(c * TILE, TILE)
                    value = product(i, j, cent, row).reshape(TILE // 8, 8, LANES)
                    before = high[:, lanes]
                    now = jnp.maximum(before, jnp.max(value, axis=0))
                    high[:, lanes] = now
                    total[:, lanes] = total[:, lanes] * jnp.exp2(before - now) + jnp.sum(
                        jnp.exp2(value - now[None]), axis=0
                    )

    top = jnp.max(high[...], axis=0, keepdims=True)
    all_sum = jnp.sum(total[...] * jnp.exp2(high[...] - top), axis=0, keepdims=True)
    out_ref[...] = top + jnp.log2(all_sum)


def score(rows, centres, plan, name, vmem, prior=None, priors=(), kept=None, keep=False):
    width = (*rows, *centres)[0].shape[1]
    rows_new = tuple(value.shape[0] for value in rows)
    cents_new = tuple(value.shape[0] for value in centres)
    kept_rows, rows_kept, kept_cents, cents_kept = kept or (None, (), None, ())
    count = sum(rows_new) + sum(rows_kept)
    out = jax.ShapeDtypeStruct((1, count), jnp.float32)
    held = [(sum(rows_new) or 16, width), (sum(cents_new) or 16, width)]
    resident = [value for value in (kept_rows, kept_cents) if value is not None]
    if prior is None:
        prior = jnp.zeros((1, 128), jnp.float32)
    return pl.pallas_call(
        functools.partial(
            score_kernel, rows_new, rows_kept, cents_new, cents_kept, tuple(priors), plan, keep
        ),
        out_shape=(out, *[jax.ShapeDtypeStruct(shape, jnp.bfloat16) for shape in held])
        if keep
        else out,
        in_specs=[ANY] * (len(rows) + len(centres)) + [VMEM] * (len(resident) + 1),
        out_specs=(VMEM,) * 3 if keep else VMEM,
        scratch_shapes=([] if keep else [pltpu.VMEM(shape, jnp.bfloat16) for shape in held])
        + [
            pltpu.VMEM((8, count), jnp.float32),
            pltpu.VMEM((8, count), jnp.float32),
            pltpu.SemaphoreType.DMA((sum(rows_new) // STEP or 1,)),
            pltpu.SemaphoreType.DMA((sum(cents_new) // STEP,)),
        ],
        compiler_params=pltpu.CompilerParams(vmem_limit_bytes=vmem * 1024 * 1024),
        cost_estimate=pl.CostEstimate(flops=1 if name == "score_far" else 1, bytes_accessed=1, transcendentals=0),
        name=name,
    )(*(map(in_hbm, (*rows, *centres)) if kept is None else (*rows, *centres)), *resident, prior)


def owner_kernel(rows_hbm, out_ref, rows_ref, sems):
    total = rows_ref.shape[0]
    width = rows_ref.shape[1] - ID_LANES
    cap = out_ref.shape[1]
    block = LANES
    copies = [
        pltpu.make_async_copy(
            rows_hbm.at[pl.ds(i * block, block)], rows_ref.at[pl.ds(i * block, block)], sems.at[i]
        )
        for i in range(total // block)
    ]
    for copy in copies:
        copy.start()
    pick = (lax.broadcasted_iota(jnp.int32, (8, ID_LANES), 1) == 0).astype(jnp.float32)
    pick = pick.astype(jnp.bfloat16)
    r = lax.broadcasted_iota(jnp.int32, (block, block), 0)
    s = lax.broadcasted_iota(jnp.int32, (block, block), 1)
    eye = lax.broadcasted_iota(jnp.int32, (cap, ID_LANES), 0)
    eye = (eye == lax.broadcasted_iota(jnp.int32, (cap, ID_LANES), 1)).astype(jnp.float32)
    id_rows = []
    for row in range(0, total, block):
        if row in (0, total // 2):
            for copy in copies[row // block : (row + total // 2) // block]:
                copy.wait()
        ids = rows_ref[row : row + block, width:]
        id_rows.append(lax.dot_general(pick, ids, NT, preferred_element_type=jnp.float32)[:1])
        id_col = ids.astype(jnp.float32)
        best = jnp.full((block, ID_LANES), -1.0, jnp.float32)
        for col in range(0, row + block, block):
            gram = lax.dot_general(
                rows_ref[row : row + block, :width],
                rows_ref[col : col + block, :width],
                NT,
                preferred_element_type=jnp.float32,
            )
            for lane in range(0, block, ID_LANES):
                lanes = slice(lane, lane + ID_LANES)
                same = id_col == id_rows[col // block][:, lanes]
                if row == col:
                    same = same & (s < r)[:, lanes]
                best = jnp.maximum(best, jnp.where(same, gram[:, lanes], -1.0))
        best = jnp.max(best, axis=1, keepdims=True).reshape(block // cap, cap, 1)
        best = jnp.sum(best * eye[None], axis=1)
        out_ref[row // cap : (row + block) // cap, :] = best[:, :cap]


def owner_best(rows, cap):
    total, width = rows.shape
    return pl.pallas_call(
        owner_kernel,
        out_shape=jax.ShapeDtypeStruct((total // cap, cap), jnp.float32),
        in_specs=[ANY],
        out_specs=VMEM,
        scratch_shapes=[
            pltpu.VMEM((total, width), jnp.bfloat16),
            pltpu.SemaphoreType.DMA((total // LANES,)),
        ],
        compiler_params=SCORE_PARAMS,
        cost_estimate=TINY,
        name="owner_best",
    )(rows)


def pick_kernel(per_owner, got_ref, cluster_ref, slot_ref, out_ref):
    got = got_ref[...]
    devices, cap = got.shape
    rows = out_ref.shape[1]
    owner = cluster_ref[...] // per_owner
    hot = (lax.broadcasted_iota(jnp.int32, (devices, rows), 0) == owner).astype(jnp.float32)
    by_slot = lax.dot_general(
        got,
        hot,
        (((0,), (0,)), ((), ())),
        precision=lax.Precision.HIGHEST,
        preferred_element_type=jnp.float32,
    )
    mine = lax.broadcasted_iota(jnp.int32, (cap, rows), 0) == slot_ref[...]
    out_ref[...] = jnp.sum(jnp.where(mine, by_slot, 0.0), axis=0, keepdims=True)


def pick(got, cluster, slot, per_owner):
    rows = cluster.shape[0]
    return pl.pallas_call(
        functools.partial(pick_kernel, per_owner),
        out_shape=jax.ShapeDtypeStruct((1, rows), jnp.float32),
        in_specs=[VMEM] * 3,
        out_specs=VMEM,
        compiler_params=SCORE_PARAMS,
        cost_estimate=TINY,
        name="pick",
    )(got, cluster.reshape(1, rows), slot.reshape(1, rows)).reshape(rows)


def move(value, step):
    pairs = []
    for y in range(4):
        for x in range(4):
            for z in range(4):
                for core in range(2):
                    here, there = [
                        (y * 2 + a % 4 // 2) * 16 + (b % 4 * 2 + a % 2) * 2 + c
                        for a, b, c in ((x, z, core), step(x, z, core))
                    ]
                    pairs.append((here, there))
    return lax.ppermute(value, ("doc", "cent"), pairs)


def swap_core(value):
    return move(value, lambda x, z, core: (x, z, 1 - core))


def move_x(value):
    return move(value, lambda x, z, core: (x + 1 - 2 * core, z, core))


def move_z(value, by):
    return move(value, lambda x, z, core: (x, z + by * (1 - 2 * core), core))


def per_device(embeddings, centroids, cluster, slot):
    row_count, width = embeddings.shape
    devices = lax.axis_size("doc") * lax.axis_size("cent")
    per_owner = centroids.shape[0] // lax.axis_size("doc")
    cap = 2 * row_count // devices

    unit, send = prepare_rows(embeddings, cluster, slot, per_owner, cap, devices)
    centre = prepare_centres(lax.optimization_barrier((centroids, unit))[0])
    ahead, behind = move_z(unit, 1), move_z(unit, -1)
    side, core = move_x(centre), swap_core(centre)
    plan = (((0,), (0,), ((0, 0),)), ((), (1,), ((1, 0),)))
    first = score((unit,), (centre, core), plan, "score_own", 24)

    def after(value, done):
        return lax.optimization_barrier((value, done))[0]

    got = lax.all_to_all(
        send.reshape(devices, cap, width + ID_LANES),
        ("doc", "cent"),
        split_axis=0,
        concat_axis=0,
        tiled=True,
    )
    best = owner_best(after(got, first).reshape(devices * cap, width + ID_LANES), cap)
    returned = lax.all_to_all(best, ("doc", "cent"), split_axis=0, concat_axis=0, tiled=True)

    side, ahead, behind = after(side, returned), after(ahead, returned), after(behind, returned)
    side_core = swap_core(after(side, (ahead, behind)))
    far = move_z(ahead, 1)
    plan = (
        ((0, 1), (0,), ((0, 0), (0, 1))),
        ((2,), (1,), ((0, 2), (1, 1), (1, 2))),
        ((), (2,), ((2, 1), (2, 2))),
    )
    near, rows, table = score(
        (unit, ahead, behind),
        (side, centre, core),
        plan,
        "score_near",
        24,
        prior=first,
        priors=(0,),
        keep=True,
    )
    plan = (((), (0,), ((0, 0), (0, 1), (0, 2))),)
    sizes = (row_count,) * 3
    mid = score(
        (), (side_core,), plan, "score_mid", 16, prior=near, priors=(0, 1, 2), kept=(rows, sizes, None, ())
    )
    parts = [mid[:, i * row_count : (i + 1) * row_count] for i in range(3)]
    plan = (((0,), (), ((1, 0), (2, 0), (3, 0))), ((), (0,), ((0, 0),)))
    kept = (None, (), table, (centre.shape[0],) * 3)
    last = score((after(far, mid),), (side_core,), plan, "score_far", 16, kept=kept)
    dup_sim = pick(after(returned, last), cluster, slot, per_owner)
    terms = (move_z(last, 2), parts[0], move_z(parts[1], -1), move_z(parts[2], 1))
    terms = jnp.concatenate(terms, axis=0)
    top = jnp.max(terms, axis=0)
    soft_cost = 1.0 - BACK * (top + jnp.log2(jnp.sum(jnp.exp2(terms - top[None]), axis=0)))
    return (soft_cost, dup_sim)


def solution(mesh):
    return jax.shard_map(
        per_device,
        mesh=mesh,
        in_specs=(
            P(("doc", "cent"), None),
            P("cent", None),
            P(("doc", "cent")),
            P(("doc", "cent")),
        ),
        out_specs=(P(("doc", "cent")), P(("doc", "cent"))),
        check_vma=False,
    )
```
